256 devices in a mesh: gx: 64 (over y, z, core), gy: 4 (over x).
Axes of the slice: x: 4, y: 4, z: 8, core: 2. Of those that a mesh axis runs over, the one named last changes fastest.
Arguments:
- query: bfloat16 [256, 16384], P('gx', 'gy'), may hold values from -48 to 48
- key_cache: bfloat16 [256, 8, 256, 128], P('gx', 'gy'), may hold values from -13 to 13
- value_cache: bfloat16 [256, 8, 256, 128], P('gx', 'gy'), may hold values from -5 to 5
- key_new: bfloat16 [256, 1024], P('gx', 'gy'), may hold values from -13 to 13
- value_new: bfloat16 [256, 1024], P('gx', 'gy'), may hold values from -5 to 5
- lengths: int32 [256], P('gx'), may hold values from 1 to 256, as said below
- residual_in: bfloat16 [256, 16384], P(None, ('gy', 'gx')), may hold values from -24 to 24
- out_weight: bfloat16 [16384, 16384], P(None, ('gy', 'gx')), may hold values from -0.046875 to 0.046875
- norm_gain: bfloat16 [16384], P(('gy', 'gx')), may hold values from 0.25 to 1.75
- gate_weight: bfloat16 [16384, 26624], P('gy', 'gx'), may hold values from -0.046875 to 0.046875
- up_weight: bfloat16 [16384, 26624], P('gy', 'gx'), may hold values from -0.046875 to 0.046875
- down_weight: bfloat16 [26624, 16384], P('gx', 'gy'), may hold values from -0.109375 to 0.109375
Outputs:
- layer_out: bfloat16 [256, 16384], P(None, ('gy', 'gx'))
The draws below stay inside these ranges and needn't reach their ends.
Inputs may be any that keep to these rules, and one draw needn't show every extreme that they name: `lengths`: some row has exactly 256 valid positions and some row exactly 1.
All inputs are finite; a program needn't handle non-finite values.
Results may differ from the reference program's by a relative error of at most 0.007.
Values may be sent and summed in bfloat16 or wider, within the bound.
No kernel may reach another device: no remote copies, remote signals or barrier semaphores. Data moves between devices by JAX's collectives and lax.ppermute only.
A program may use at most 128 MiB of HBM per device.

```python
import math
import jax
import jax.numpy as jnp
from jax import lax

D = 16384
HQ = 128
KVH = 8
HD = 128
FF = 26624
CTX = 256
ROWS = 256


def draw_query(key, part):
    key = jax.random.fold_in(key, 1)
    values = jnp.clip(jax.random.normal(key, (ROWS, HQ * HD), jnp.float32), -4.0, 4.0)
    return values.astype(jnp.bfloat16)


def draw_key_cache(key, part):
    key = jax.random.fold_in(key, 2)
    values = jnp.clip(jax.random.normal(key, (ROWS, KVH, CTX, HD), jnp.float32), -4.0, 4.0)
    return values.astype(jnp.bfloat16)


def draw_key_new(key, part):
    key = jax.random.fold_in(key, 3)
    values = jnp.clip(jax.random.normal(key, (ROWS, KVH * HD), jnp.float32), -4.0, 4.0)
    return values.astype(jnp.bfloat16)


def draw_residual_in(key, part):
    key = jax.random.fold_in(key, 4)
    column = jnp.arange(D).astype(jnp.float32) / D
    column_scale = 0.25 * jnp.exp(math.log(10.0) * column)
    row_scale = jnp.exp(jax.random.uniform(jax.random.fold_in(key, 2), (ROWS, 1), jnp.float32, math.log(0.5), math.log(2.0)))
    noise = jnp.clip(jax.random.normal(jax.random.fold_in(key, 1), (ROWS, D), jnp.float32), -4.0, 4.0)
    return (noise * row_scale * column_scale[None, :]).astype(jnp.bfloat16)


def draw_lengths(key, part):
    key = jax.random.fold_in(key, 5)
    drawn = jax.random.randint(jax.random.fold_in(key, 1), (ROWS,), 1, CTX + 1)
    longest = jax.random.randint(jax.random.fold_in(key, 2), (), 0, ROWS)
    shortest = (longest + 1) % ROWS
    positions = jnp.arange(ROWS)
    drawn = jnp.where(positions == longest, CTX, drawn)
    drawn = jnp.where(positions == shortest, 1, drawn)
    return drawn.astype(jnp.int32)


def strengthened(result, own_key, source, target, blocks, factor):
    owner, partner = [(jnp.arange(result.shape[axis_at]) // (result.shape[axis_at] // blocks)).reshape([-1 if axis == axis_at else 1 for axis in range(result.ndim)]) for axis_at in (source, target)]
    chosen = jax.random.permutation(own_key, blocks)[partner]
    strong = (owner == chosen) | (owner == (partner + blocks // 2) % blocks)
    return jnp.where(strong, factor * result, result)


def levels(key, dims, shards, smallest, largest):
    def one(dim, blocks):
        heights = jax.random.uniform(jax.random.fold_in(jax.random.fold_in(key, 6), dim), (blocks,), jnp.float32, smallest / len(shards), largest / len(shards))
        return jnp.repeat(jnp.exp(heights), dims[dim] // blocks).reshape((-1,) + (1,) * (len(dims) - dim - 1))

    factor_of = one(*shards[0])
    for cut in shards[1:]:
        factor_of = factor_of * one(*cut)
    return factor_of


def bell_draw(rng, dims, spread, limit, shards=(), kind=jnp.bfloat16):
    array = spread * jax.random.normal(rng, dims, jnp.float32)
    if shards:
        array = array * levels(rng, dims, shards, -0.22, 0.18)
    return jnp.clip(array, -limit, limit).astype(kind)


def heavy_noise(key, shape, deviation, most, cuts, heavy, held_as=jnp.bfloat16):
    array = deviation * jax.random.normal(key, shape, jnp.float32)
    if cuts:
        array = array * levels(key, shape, cuts, -0.22, 0.18)
    return jnp.clip(strengthened(array, jax.random.fold_in(key, 3), *heavy), -most, most).astype(held_as)


def setup_inputs(seed: int = 0) -> dict:
    keys = jax.random.split(jax.random.key(seed), 13)
    return {
        "query": draw_query(jax.random.fold_in(keys[12], 71), 0),
        "key_cache": draw_key_cache(jax.random.fold_in(keys[12], 71), 0),
        "value_cache": bell_draw(keys[2], (ROWS, KVH, CTX, HD), 1.0, 5.0, ((0, 64), (1, 4))),
        "key_new": draw_key_new(jax.random.fold_in(keys[12], 71), 0),
        "value_new": bell_draw(keys[4], (ROWS, KVH * HD), 1.0, 5.0, ((0, 64), (1, 4))),
        "lengths": draw_lengths(jax.random.fold_in(keys[12], 71), 0),
        "residual_in": draw_residual_in(jax.random.fold_in(keys[12], 71), 0),
        "out_weight": bell_draw(keys[7], (HQ * HD, D), (HQ * HD) ** -0.5, 0.046875, ((1, 256),)),
        "norm_gain": jnp.clip(1.0 + 0.15 * jax.random.normal(keys[8], (D,), jnp.float32), 0.25, 1.75).astype(jnp.bfloat16),
        "gate_weight": bell_draw(keys[9], (D, FF), D ** -0.5, 0.046875, ((0, 4), (1, 64))),
        "up_weight": bell_draw(keys[10], (D, FF), D ** -0.5, 0.046875, ((0, 4), (1, 64))),
        "down_weight": heavy_noise(keys[11], (FF, D), FF ** -0.5, 0.109375, ((0, 64), (1, 4)), (0, 1, 64, 4.0)),
    }


def attention(query, key_cache, value_cache, key_new, value_new, lengths):
    row_count = query.shape[0]
    kv_heads = key_cache.shape[1]
    context = key_cache.shape[2]
    head_size = key_cache.shape[3]
    group_size = query.shape[1] // (kv_heads * head_size)
    query_rows = query.astype(jnp.float32).reshape(row_count, kv_heads, group_size, head_size)
    incoming_keys = key_new.astype(jnp.float32).reshape(row_count, kv_heads, head_size)
    fresh_values = value_new.astype(jnp.float32).reshape(row_count, kv_heads, head_size)
    logit_scale = head_size ** (-0.5)
    cache_scores = jnp.einsum('bkgd,bktd->bkgt', query_rows, key_cache.astype(jnp.float32)) * logit_scale
    incoming_scores = jnp.einsum('qaxh,qah->qax', query_rows, incoming_keys) * logit_scale
    valid = lax.broadcasted_iota(jnp.int32, (row_count, context), 1) < lengths.astype(jnp.int32)[:, None]
    cache_scores = jnp.where(valid[:, None, None, :], cache_scores, -1e+30)
    peak = jnp.maximum(lax.optimization_barrier(jnp.max(cache_scores, axis=3)), incoming_scores)
    cache_weights = jnp.exp(cache_scores - peak[..., None])
    new_weight = jnp.exp(incoming_scores - peak)
    denominator = lax.optimization_barrier(jnp.sum(cache_weights, axis=3)) + new_weight
    cache_low = lax.optimization_barrier(cache_weights.astype(jnp.bfloat16)).astype(jnp.float32)
    new_low = lax.optimization_barrier(new_weight.astype(jnp.bfloat16)).astype(jnp.float32)
    weighted_value_sum = jnp.einsum('bkgt,bktd->bkgd', cache_low, value_cache.astype(jnp.float32))
    weighted_value_sum = weighted_value_sum + new_low[..., None] * fresh_values[:, :, None, :]
    attended = (weighted_value_sum / denominator[..., None]).astype(jnp.bfloat16)
    return attended.reshape(row_count, kv_heads * group_size * head_size)

def reference(query, key_cache, value_cache, key_new, value_new, lengths, residual_in, out_weight, norm_gain, gate_weight, up_weight, down_weight):
    attended = attention(query, key_cache, value_cache, key_new, value_new, lengths)
    projected = jnp.dot(attended, out_weight, preferred_element_type=jnp.float32)
    hsum = residual_in.astype(jnp.float32) + projected
    mean_square = lax.optimization_barrier(jnp.mean(hsum * hsum, axis=1, keepdims=True))
    normed = (hsum * lax.rsqrt(mean_square + 1e-05) * norm_gain.astype(jnp.float32)[None, :]).astype(jnp.bfloat16)
    gate = jnp.dot(normed, gate_weight, preferred_element_type=jnp.float32)
    up = jnp.dot(normed, up_weight, preferred_element_type=jnp.float32)
    hidden = (jax.nn.silu(gate) * up).astype(jnp.bfloat16)
    branch = jnp.dot(hidden, down_weight, preferred_element_type=jnp.float32)
    return (hsum + branch).astype(jnp.bfloat16)
```

```python
import jax
import jax.numpy as jnp
import numpy as np
from jax import lax
from jax.sharding import PartitionSpec as P

D = 16384
PLANE = 32
CORES = 2
QUARTERS = 4
ROWS_HERE = 4

F32 = jnp.float32
BF16 = jnp.bfloat16


def row_order():
    row = np.arange(PLANE * CORES * ROWS_HERE)
    device, inner = row // ROWS_HERE, row % ROWS_HERE
    place = (device % CORES) * (PLANE * ROWS_HERE) + (device // CORES) * ROWS_HERE + inner
    table = np.zeros((row.size, row.size), np.float32)
    table[row, place] = 1.0
    return table


def to_core(value):
    return lax.ppermute(value, "gx", [(g, g ^ 1) for g in range(PLANE * CORES)])


def along_gy(value, step):
    return lax.ppermute(value, "gy", [(i, (i + step) % QUARTERS) for i in range(QUARTERS)])


def plane_exchange(blocks):
    groups = [[p * CORES + c for p in range(PLANE)] for c in range(CORES)]
    return lax.all_to_all(blocks, "gx", 0, 0, axis_index_groups=groups, tiled=True)


def attend(query, key_cache, value_cache, key_new, value_new, lengths):
    row_count = query.shape[0]
    kv_heads = key_cache.shape[1]
    context = key_cache.shape[2]
    head_size = key_cache.shape[3]
    group_size = query.shape[1] // (kv_heads * head_size)
    query_rows = query.reshape(row_count, kv_heads, group_size, head_size)
    incoming_keys = key_new.reshape(row_count, kv_heads, head_size)
    fresh_values = value_new.astype(F32).reshape(row_count, kv_heads, head_size)
    logit_scale = head_size ** (-0.5)
    cache_scores = (
        jnp.einsum("bkgd,bktd->bkgt", query_rows, key_cache, preferred_element_type=F32)
        * logit_scale
    )
    incoming_scores = (
        jnp.einsum("qaxh,qah->qax", query_rows, incoming_keys, preferred_element_type=F32)
        * logit_scale
    )
    valid = lax.broadcasted_iota(jnp.int32, (row_count, context), 1) < lengths[:, None]
    cache_scores = jnp.where(valid[:, None, None, :], cache_scores, -1e30)
    peak = jnp.maximum(jnp.max(cache_scores, axis=3), incoming_scores)
    cache_weights = jnp.exp(cache_scores - peak[..., None])
    new_weight = jnp.exp(incoming_scores - peak)
    denominator = jnp.sum(cache_weights, axis=3) + new_weight
    cache_low = cache_weights.astype(BF16)
    new_low = new_weight.astype(BF16).astype(F32)
    weighted_value_sum = jnp.einsum(
        "bkgt,bktd->bkgd", cache_low, value_cache, preferred_element_type=F32
    )
    weighted_value_sum = weighted_value_sum + new_low[..., None] * fresh_values[:, :, None, :]
    attended = (weighted_value_sum / denominator[..., None]).astype(BF16)
    return attended.reshape(row_count, kv_heads * group_size * head_size)


def pair_order(own, other, core):
    return jnp.where(
        core == 0, jnp.concatenate([own, other], 0), jnp.concatenate([other, own], 0)
    )


def per_device(
    query,
    key_cache,
    value_cache,
    key_new,
    value_new,
    lengths,
    residual_in,
    out_weight,
    norm_gain,
    gate_weight,
    up_weight,
    down_weight,
):
    core = lax.axis_index("gx") % CORES
    quarter = lax.axis_index("gy")
    order = jnp.asarray(row_order(), BF16)
    width = out_weight.shape[0] // QUARTERS
    columns = out_weight.shape[1]
    half = PLANE * ROWS_HERE

    out_rows = out_weight.T
    own_out = [lax.dynamic_slice_in_dim(out_rows, quarter * width, width, 1)]
    for step in range(1, QUARTERS):
        to = (quarter + step) % QUARTERS
        own_out.append(along_gy(lax.dynamic_slice_in_dim(out_rows, to * width, width, 1), step))
    own_out = jnp.concatenate(own_out, 0)

    gate_other, up_other = to_core(gate_weight.T), to_core(up_weight.T)
    down_other = to_core(down_weight)

    residual = jnp.dot(residual_in.T, order, preferred_element_type=F32).astype(BF16)
    gain = jnp.broadcast_to(norm_gain[:, None], (columns, half))
    mine = lax.dynamic_slice_in_dim(residual, core * half, half, 1)
    theirs = lax.dynamic_slice_in_dim(residual, (1 - core) * half, half, 1)
    received = to_core(jnp.concatenate([theirs, gain], 1))
    residual = pair_order(mine, received[:, :half], core).astype(F32)
    gain = pair_order(gain, received[:, half:], core).astype(F32)

    attended = attend(query, key_cache, value_cache, key_new, value_new, lengths)
    gathered = plane_exchange(jnp.broadcast_to(attended[None], (PLANE,) + attended.shape))
    rows = gathered.reshape(half, width)

    other_out = to_core(own_out)

    def project(weights):
        return lax.dot_general(
            weights, rows, (((1,), (1,)), ((), ())), preferred_element_type=F32
        ).reshape(QUARTERS, columns, half)

    own_part, other_part = project(own_out), project(other_out)
    parts = jnp.where(
        core == 0,
        jnp.concatenate([own_part, other_part], 1),
        jnp.concatenate([other_part, own_part], 1),
    )
    projected = parts[0]
    for step in range(1, QUARTERS):
        projected = projected + along_gy(parts[step].astype(BF16), -step).astype(F32)
    hsum = residual + projected

    squares = jnp.sum(hsum * hsum, axis=0, keepdims=True)
    high = squares.astype(BF16)
    low = (squares - high.astype(F32)).astype(BF16)
    block = jnp.concatenate(
        [(hsum * gain).astype(BF16), high, low, jnp.zeros((14, half), BF16)], 0
    )
    blocks = plane_exchange(jnp.broadcast_to(block[None], (PLANE,) + block.shape))
    features = blocks[:, : CORES * columns].reshape(width, half)
    squares = jnp.sum(blocks[:, 128].astype(F32) + blocks[:, 129].astype(F32), axis=0)

    units = gate_weight.shape[1] // 2
    def expand(weights):
        return jnp.dot(weights, features, preferred_element_type=F32).reshape(2, units, half)

    gates = jnp.concatenate([expand(gate_weight.T), expand(gate_other)], 0)
    ups = jnp.concatenate([expand(up_weight.T), expand(up_other)], 0)
    high = squares.astype(BF16)
    low = (squares - high.astype(F32)).astype(BF16)
    tail = jnp.concatenate([high[None], low[None], jnp.zeros((14, half), BF16)], 0)
    tail = jnp.broadcast_to(tail[None], (QUARTERS,) + tail.shape)
    sends = jnp.concatenate([gates.astype(BF16), ups.astype(BF16), tail], 1)

    def chunk_of(to):
        return ((to // 2) ^ core) * 2 + to % 2

    total = lax.dynamic_index_in_dim(sends, chunk_of(quarter), 0, False).astype(F32)
    for step in range(1, QUARTERS):
        to = (quarter + step) % QUARTERS
        part = lax.dynamic_index_in_dim(sends, chunk_of(to), 0, False)
        total = total + along_gy(part, step).astype(F32)
    squares = total[2 * units : 2 * units + 1] + total[2 * units + 1 : 2 * units + 2]
    inverse = lax.rsqrt(squares / D + 1e-05)
    gate = total[:units] * inverse
    up = total[units : 2 * units] * inverse
    hidden = (jax.nn.silu(gate) * up).astype(BF16)

    chunks = jnp.stack([hidden] + [along_gy(hidden, step) for step in range(1, QUARTERS)])
    ordered = [
        lax.dynamic_index_in_dim(
            chunks, (quarter - (((place // 2) ^ core) * 2 + place % 2)) % QUARTERS, 0, False
        )
        for place in range(QUARTERS)
    ]
    hidden = jnp.concatenate(ordered, 0)

    def contract(weights, values):
        return lax.dot_general(
            weights, values, (((0,), (0,)), ((), ())), preferred_element_type=F32
        )

    branch = contract(down_weight, hidden[: 2 * units]) + contract(down_other, hidden[2 * units :])
    branch = branch.astype(BF16).reshape(PLANE, CORES * columns, half)
    branch = jnp.sum(plane_exchange(branch).astype(F32), axis=0)

    out = (hsum + branch).astype(BF16)
    mine = lax.dynamic_slice_in_dim(out, core * columns, columns, 0)
    theirs = to_core(lax.dynamic_slice_in_dim(out, (1 - core) * columns, columns, 0))
    out = jnp.where(
        core == 0,
        jnp.concatenate([mine, theirs], 1),
        jnp.concatenate([theirs, mine], 1),
    )
    out = lax.dot_general(order, out, (((1,), (1,)), ((), ())), preferred_element_type=F32)
    return out.astype(BF16)


def solution(mesh):
    placed = (
        P("gx", "gy"),
        P("gx", "gy", None, None),
        P("gx", "gy", None, None),
        P("gx", "gy"),
        P("gx", "gy"),
        P("gx"),
        P(None, ("gy", "gx")),
        P(None, ("gy", "gx")),
        P(("gy", "gx")),
        P("gy", "gx"),
        P("gy", "gx"),
        P("gx", "gy"),
    )
    return jax.shard_map(
        per_device, mesh=mesh, in_specs=placed, out_specs=P(None, ("gy", "gx")), check_vma=False
    )
```

```python
import jax
import jax.numpy as jnp
import numpy as np
from jax import lax
from jax.experimental import pallas as pl
from jax.experimental.pallas import tpu as pltpu
from jax.sharding import PartitionSpec as P

D = 16384
PLANE = 32
CORES = 2
QUARTERS = 4
ROWS_HERE = 4
HALF = PLANE * ROWS_HERE
PAIR = 128
PARTS = 2
TAIL = 16

F32 = jnp.float32
BF16 = jnp.bfloat16


def row_order():
    row = np.arange(PLANE * CORES * ROWS_HERE)
    device, inner = row // ROWS_HERE, row % ROWS_HERE
    place = (device % CORES) * (PLANE * ROWS_HERE) + (device // CORES) * ROWS_HERE + inner
    table = np.zeros((row.size, row.size), np.float32)
    table[row, place] = 1.0
    return table


def to_core(value):
    return lax.ppermute(value, "gx", [(g, g ^ 1) for g in range(PLANE * CORES)])


def along_gy(value, step):
    return lax.ppermute(value, "gy", [(i, (i + step) % QUARTERS) for i in range(QUARTERS)])


def plane_exchange(blocks):
    groups = [[p * CORES + c for p in range(PLANE)] for c in range(CORES)]
    return lax.all_to_all(blocks, "gx", 0, 0, axis_index_groups=groups, tiled=True)


def attend(query, key_cache, value_cache, key_new, value_new, lengths):
    row_count = query.shape[0]
    kv_heads = key_cache.shape[1]
    context = key_cache.shape[2]
    head_size = key_cache.shape[3]
    group_size = query.shape[1] // (kv_heads * head_size)
    query_rows = query.reshape(row_count, kv_heads, group_size, head_size)
    incoming_keys = key_new.reshape(row_count, kv_heads, head_size)
    fresh_values = value_new.astype(F32).reshape(row_count, kv_heads, head_size)
    logit_scale = head_size ** (-0.5)
    cache_scores = (
        jnp.einsum("bkgd,bktd->bkgt", query_rows, key_cache, preferred_element_type=F32)
        * logit_scale
    )
    incoming_scores = (
        jnp.einsum("qaxh,qah->qax", query_rows, incoming_keys, preferred_element_type=F32)
        * logit_scale
    )
    valid = lax.broadcasted_iota(jnp.int32, (row_count, context), 1) < lengths[:, None]
    cache_scores = jnp.where(valid[:, None, None, :], cache_scores, -1e30)
    peak = jnp.maximum(jnp.max(cache_scores, axis=3), incoming_scores)
    cache_weights = jnp.exp(cache_scores - peak[..., None])
    new_weight = jnp.exp(incoming_scores - peak)
    denominator = jnp.sum(cache_weights, axis=3) + new_weight
    cache_low = cache_weights.astype(BF16)
    new_low = new_weight.astype(BF16).astype(F32)
    weighted_value_sum = jnp.einsum(
        "bkgt,bktd->bkgd", cache_low, value_cache, preferred_element_type=F32
    )
    weighted_value_sum = weighted_value_sum + new_low[..., None] * fresh_values[:, :, None, :]
    attended = (weighted_value_sum / denominator[..., None]).astype(BF16)
    return attended.reshape(row_count, kv_heads * group_size * head_size)


VMEM = pl.BlockSpec(memory_space=pltpu.VMEM)
SMEM = pl.BlockSpec(memory_space=pltpu.SMEM)
HBM = pl.BlockSpec(memory_space=pltpu.HBM)


def kernel_call(body, outs, scratch=(), scalars=1, streamed=0, inputs=0, limit=8):
    return pl.pallas_call(
        body,
        out_shape=outs,
        in_specs=[SMEM] * scalars + [HBM] * streamed + [VMEM] * inputs,
        out_specs=[VMEM] * len(outs),
        scratch_shapes=list(scratch),
        compiler_params=pltpu.CompilerParams(vmem_limit_bytes=limit * 2**20),
    )


def held(value):
    return pltpu.with_memory_space_constraint(value, pltpu.VMEM)


def halves(source, target, sems):
    rows = source.shape[0] // PARTS
    return [
        pltpu.make_async_copy(
            source.at[pl.ds(part * rows, rows)], target.at[pl.ds(part * rows, rows)], sems.at[part]
        )
        for part in range(PARTS)
    ]


def run_copies(copies):
    for copy in copies:
        copy.start()
    for copy in copies:
        copy.wait()


def cut_kernel(place_ref, weights_ref, *refs):
    outs, sems = refs[:-1], refs[-1]
    width = outs[0].shape[1]
    copies = []
    for step, out in enumerate(outs, 1):
        start = pl.multiple_of(lax.rem(place_ref[0] + step, QUARTERS) * width, width)
        copies.append(
            pltpu.make_async_copy(
                weights_ref.at[:, pl.ds(start, width)], out, sems.at[step - 1]
            )
        )
    run_copies(copies)


def cut(place, weights, width):
    piece = jax.ShapeDtypeStruct((weights.shape[0], width), weights.dtype)
    return pl.pallas_call(
        cut_kernel,
        out_shape=[piece] * (QUARTERS - 1),
        in_specs=[SMEM, HBM],
        out_specs=[VMEM] * (QUARTERS - 1),
        scratch_shapes=[pltpu.SemaphoreType.DMA((QUARTERS - 1,))],
    )(place, in_hbm(weights))


def in_hbm(value):
    return pltpu.with_memory_space_constraint(value, pltpu.HBM)


def load_kernel(*refs):
    count, sems = len(refs) // 2, refs[-1]
    run_copies(
        [
            copy
            for place in range(count)
            for copy in halves(refs[place], refs[count + place], sems.at[place])
        ]
    )


def loaded(*values):
    return pl.pallas_call(
        load_kernel,
        out_shape=[pltpu.VMEM(v.shape, v.dtype) for v in values],
        in_specs=[HBM] * len(values),
        out_specs=[VMEM] * len(values),
        scratch_shapes=[pltpu.SemaphoreType.DMA((len(values), PARTS))],
        compiler_params=pltpu.CompilerParams(vmem_limit_bytes=2 * 2**20),
    )(*[in_hbm(v) for v in values])


def spread(squares):
    high = squares.astype(BF16)
    low = (squares - high.astype(F32)).astype(BF16)
    row = lax.broadcasted_iota(jnp.int32, (TAIL, squares.shape[1]), 0)
    high, low = high.astype(F32), low.astype(F32)
    return jnp.where(row == 0, high, jnp.where(row == 1, low, 0.0)).astype(BF16)


def hsum_kernel(own_ref, a_ref, b_ref, c_ref, residual_ref, gain_ref, hsum_ref, blocks_ref):
    hsum = (
        residual_ref[...].astype(F32)
        + own_ref[...]
        + a_ref[...].astype(F32)
        + b_ref[...].astype(F32)
        + c_ref[...].astype(F32)
    )
    hsum_ref[...] = hsum
    scaled = (hsum * gain_ref[...].astype(F32)).astype(BF16)
    tail = spread(jnp.sum(hsum * hsum, axis=0, keepdims=True))
    for p in range(PLANE):
        blocks_ref[p, :PAIR, :] = scaled
        blocks_ref[p, PAIR:, :] = tail


def expand_kernel(a_step, b_step, c_step, d_step, *refs):
    weights, blocks_ref, outs = refs[:4], refs[4], refs[5 : 5 + QUARTERS]
    features, sums, buffer, sems = refs[5 + QUARTERS :]
    copies = [
        halves(ref, buffer.at[place], sems.at[place]) for place, ref in enumerate(weights)
    ]
    for group in copies:
        for copy in group:
            copy.start()
    steps = [ref[0] for ref in (a_step, b_step, c_step, d_step)]
    units = weights[0].shape[0] // 2
    squares = jnp.zeros((TAIL, HALF), F32)
    for p in range(PLANE):
        features[p * PAIR : (p + 1) * PAIR, :] = blocks_ref[p, :PAIR, :]
        squares = squares + blocks_ref[p, PAIR:, :].astype(F32)
    tail = spread(squares[0:1] + squares[1:2])
    for place, group in enumerate(copies):
        for copy in group:
            copy.wait()
        sums[place * 2 * units : (place + 1) * 2 * units, :] = jnp.dot(
            buffer[place], features[...], preferred_element_type=F32
        )
    for part in range(QUARTERS):
        start = (part // 2 * 4 + part % 2) * units
        gates, ups = slice(start, start + units), slice(start + 2 * units, start + 3 * units)
        for step in range(QUARTERS):

            @pl.when(steps[part] == step)
            def _(gates=gates, ups=ups, step=step):
                outs[step][:units, :] = sums[gates, :].astype(BF16)
                outs[step][units : 2 * units, :] = sums[ups, :].astype(BF16)
                outs[step][2 * units :, :] = tail


def hidden_kernel(a_ref, b_ref, c_ref, d_ref, hidden_ref):
    units = hidden_ref.shape[0]
    total = a_ref[...].astype(F32) + b_ref[...].astype(F32)
    total = total + c_ref[...].astype(F32) + d_ref[...].astype(F32)
    squares = total[2 * units : 2 * units + 1] + total[2 * units + 1 : 2 * units + 2]
    inverse = lax.rsqrt(squares / D + 1e-05)
    gate = total[:units] * inverse
    up = total[units : 2 * units] * inverse
    hidden_ref[...] = (gate / (1.0 + jnp.exp(-gate)) * up).astype(BF16)


def contract_kernel(places_ref, own_ref, other_ref, a_ref, b_ref, c_ref, d_ref, out_ref, hidden):
    for step, ref in enumerate((a_ref, b_ref, c_ref, d_ref)):
        start = pl.multiple_of(places_ref[step] * ref.shape[0], 16)
        hidden[pl.ds(start, ref.shape[0]), :] = ref[...]
    values = hidden[...].astype(F32).T.astype(BF16)
    for p in range(0, PLANE, 2):
        columns = slice(p * PAIR, (p + 2) * PAIR)
        rows = jnp.concatenate([own_ref[:, columns], other_ref[:, columns]], 0)
        part = jnp.dot(values, rows, preferred_element_type=F32).astype(BF16)
        out_ref[p] = part[:, :PAIR]
        out_ref[p + 1] = part[:, PAIR:]


def pair_order(own, other, core):
    return jnp.where(
        core == 0, jnp.concatenate([own, other], 0), jnp.concatenate([other, own], 0)
    )


def per_device(
    query,
    key_cache,
    value_cache,
    key_new,
    value_new,
    lengths,
    residual_in,
    out_weight,
    norm_gain,
    gate_weight,
    up_weight,
    down_weight,
):
    core = lax.axis_index("gx") % CORES
    quarter = lax.axis_index("gy")
    order = jnp.asarray(row_order(), BF16)
    width = out_weight.shape[0] // QUARTERS
    columns = out_weight.shape[1]
    half = PLANE * ROWS_HERE

    out_rows = out_weight.T
    own_out = [lax.dynamic_slice_in_dim(out_rows, quarter * width, width, 1)]
    pieces = cut(quarter.astype(jnp.int32).reshape(1), out_rows, width)
    own_out += [along_gy(piece, step) for step, piece in enumerate(pieces, 1)]
    own_out = jnp.concatenate(own_out, 0)

    gate_other, up_other = to_core(gate_weight.T), to_core(up_weight.T)
    down_other = to_core(down_weight)

    residual = jnp.dot(residual_in.T, order, preferred_element_type=F32).astype(BF16)
    gain = jnp.broadcast_to(norm_gain[:, None], (columns, half))
    mine = lax.dynamic_slice_in_dim(residual, core * half, half, 1)
    theirs = lax.dynamic_slice_in_dim(residual, (1 - core) * half, half, 1)
    received = to_core(jnp.concatenate([theirs, gain], 1))
    residual = pair_order(mine, received[:, :half], core)
    gain = pair_order(gain, received[:, half:], core)

    attended = attend(query, key_cache, value_cache, key_new, value_new, lengths)
    gathered = plane_exchange(jnp.broadcast_to(attended[None], (PLANE,) + attended.shape))
    rows = gathered.reshape(half, width)

    other_out = to_core(own_out)

    def project(weights):
        return lax.dot_general(
            weights, rows, (((1,), (1,)), ((), ())), preferred_element_type=F32
        ).reshape(QUARTERS, columns, half)

    own_part, other_part = project(own_out), project(other_out)
    parts = jnp.where(
        core == 0,
        jnp.concatenate([own_part, other_part], 1),
        jnp.concatenate([other_part, own_part], 1),
    )
    sums = [parts[0]] + [
        along_gy(parts[step].astype(BF16), -step) for step in range(1, QUARTERS)
    ]
    hsum, blocks = kernel_call(
        hsum_kernel,
        [
            jax.ShapeDtypeStruct((PAIR, HALF), F32),
            jax.ShapeDtypeStruct((PLANE, PAIR + TAIL, HALF), BF16),
        ],
        scalars=0,
        inputs=6,
    )(*sums, residual, gain)

    steps = [
        ((((part // 2) ^ core) * 2 + part % 2 - quarter) % QUARTERS).reshape(1)
        for part in range(QUARTERS)
    ]
    blocks = plane_exchange(blocks)
    units = gate_weight.shape[1] // 2
    message = jax.ShapeDtypeStruct((2 * units + TAIL, HALF), BF16)
    sends = kernel_call(
        expand_kernel,
        [message] * QUARTERS,
        scratch=[
            pltpu.VMEM((width, HALF), BF16),
            pltpu.VMEM((8 * units, HALF), F32),
            pltpu.VMEM((4, 2 * units, width), BF16),
            pltpu.SemaphoreType.DMA((4, PARTS)),
        ],
        scalars=QUARTERS,
        streamed=4,
        inputs=1,
        limit=22,
    )(
        *steps,
        in_hbm(gate_weight.T),
        in_hbm(up_weight.T),
        in_hbm(gate_other),
        in_hbm(up_other),
        held(blocks),
    )
    sends = [sends[0]] + [along_gy(sends[step], step) for step in range(1, QUARTERS)]
    (hidden,) = kernel_call(
        hidden_kernel, [jax.ShapeDtypeStruct((units, HALF), BF16)], scalars=0, inputs=4
    )(*sends)
    chunks = [hidden] + [along_gy(hidden, step) for step in range(1, QUARTERS)]
    source = (quarter - jnp.arange(QUARTERS, dtype=jnp.int32)) % QUARTERS
    places = ((source // 2) ^ core) * 2 + source % 2
    (branch,) = kernel_call(
        contract_kernel,
        [jax.ShapeDtypeStruct((PLANE, HALF, PAIR), BF16)],
        scratch=[pltpu.VMEM((4 * units, HALF), BF16)],
        inputs=6,
    )(places, *[held(w) for w in loaded(down_weight, down_other)], *chunks)
    branch = jnp.sum(plane_exchange(branch).astype(F32), axis=0)

    out = (hsum + branch.T).astype(BF16)
    mine = lax.dynamic_slice_in_dim(out, core * columns, columns, 0)
    theirs = to_core(lax.dynamic_slice_in_dim(out, (1 - core) * columns, columns, 0))
    out = jnp.where(
        core == 0,
        jnp.concatenate([mine, theirs], 1),
        jnp.concatenate([theirs, mine], 1),
    )
    out = lax.dot_general(order, out, (((1,), (1,)), ((), ())), preferred_element_type=F32)
    return out.astype(BF16)


def solution(mesh):
    placed = (
        P("gx", "gy"),
        P("gx", "gy", None, None),
        P("gx", "gy", None, None),
        P("gx", "gy"),
        P("gx", "gy"),
        P("gx"),
        P(None, ("gy", "gx")),
        P(None, ("gy", "gx")),
        P(("gy", "gx")),
        P("gy", "gx"),
        P("gy", "gx"),
        P("gx", "gy"),
    )
    return jax.shard_map(
        per_device, mesh=mesh, in_specs=placed, out_specs=P(None, ("gy", "gx")), check_vma=False
    )
```

```python
import jax
import jax.numpy as jnp
import numpy as np
from jax import lax
from jax.experimental import pallas as pl
from jax.experimental.pallas import tpu as pltpu
from jax.sharding import PartitionSpec as P

D = 16384
PLANE = 32
CORES = 2
QUARTERS = 4
ROWS_HERE = 4
HALF = PLANE * ROWS_HERE
PAIR = 128
PARTS = 2
TAIL = 16

F32 = jnp.float32
BF16 = jnp.bfloat16


def row_order():
    row = np.arange(PLANE * CORES * ROWS_HERE)
    device, inner = row // ROWS_HERE, row % ROWS_HERE
    place = (device % CORES) * (PLANE * ROWS_HERE) + (device // CORES) * ROWS_HERE + inner
    table = np.zeros((row.size, row.size), np.float32)
    table[row, place] = 1.0
    return table


def to_core(value):
    return lax.ppermute(value, "gx", [(g, g ^ 1) for g in range(PLANE * CORES)])


def along_gy(value, step):
    return lax.ppermute(value, "gy", [(i, (i + step) % QUARTERS) for i in range(QUARTERS)])


def plane_exchange(blocks):
    groups = [[p * CORES + c for p in range(PLANE)] for c in range(CORES)]
    return lax.all_to_all(blocks, "gx", 0, 0, axis_index_groups=groups, tiled=True)


def attend(query, key_cache, value_cache, key_new, value_new, lengths):
    row_count = query.shape[0]
    kv_heads = key_cache.shape[1]
    context = key_cache.shape[2]
    head_size = key_cache.shape[3]
    group_size = query.shape[1] // (kv_heads * head_size)
    query_rows = query.reshape(row_count, kv_heads, group_size, head_size)
    incoming_keys = key_new.reshape(row_count, kv_heads, head_size)
    fresh_values = value_new.astype(F32).reshape(row_count, kv_heads, head_size)
    logit_scale = head_size ** (-0.5)
    cache_scores = (
        jnp.einsum("bkgd,bktd->bkgt", query_rows, key_cache, preferred_element_type=F32)
        * logit_scale
    )
    incoming_scores = (
        jnp.einsum("qaxh,qah->qax", query_rows, incoming_keys, preferred_element_type=F32)
        * logit_scale
    )
    valid = lax.broadcasted_iota(jnp.int32, (row_count, context), 1) < lengths[:, None]
    cache_scores = jnp.where(valid[:, None, None, :], cache_scores, -1e30)
    peak = jnp.maximum(jnp.max(cache_scores, axis=3), incoming_scores)
    cache_weights = jnp.exp(cache_scores - peak[..., None])
    new_weight = jnp.exp(incoming_scores - peak)
    denominator = jnp.sum(cache_weights, axis=3) + new_weight
    cache_low = cache_weights.astype(BF16)
    new_low = new_weight.astype(BF16).astype(F32)
    weighted_value_sum = jnp.einsum(
        "bkgt,bktd->bkgd", cache_low, value_cache, preferred_element_type=F32
    )
    weighted_value_sum = weighted_value_sum + new_low[..., None] * fresh_values[:, :, None, :]
    attended = (weighted_value_sum / denominator[..., None]).astype(BF16)
    return attended.reshape(row_count, kv_heads * group_size * head_size)


VMEM = pl.BlockSpec(memory_space=pltpu.VMEM)
SMEM = pl.BlockSpec(memory_space=pltpu.SMEM)
HBM = pl.BlockSpec(memory_space=pltpu.HBM)


def kernel_call(body, outs, scratch=(), scalars=1, streamed=0, inputs=0, limit=8):
    return pl.pallas_call(
        body,
        out_shape=outs,
        in_specs=[SMEM] * scalars + [HBM] * streamed + [VMEM] * inputs,
        out_specs=[VMEM] * len(outs),
        scratch_shapes=list(scratch),
        compiler_params=pltpu.CompilerParams(vmem_limit_bytes=limit * 2**20),
    )


def held(value):
    return pltpu.with_memory_space_constraint(value, pltpu.VMEM)


def halves(source, target, sems):
    rows = source.shape[0] // PARTS
    return [
        pltpu.make_async_copy(
            source.at[pl.ds(part * rows, rows)], target.at[pl.ds(part * rows, rows)], sems.at[part]
        )
        for part in range(PARTS)
    ]


def run_copies(copies):
    for copy in copies:
        copy.start()
    for copy in copies:
        copy.wait()


def cut_kernel(place_ref, weights_ref, *refs):
    outs, sems = refs[:-1], refs[-1]
    width = outs[0].shape[1]
    copies = []
    for step, out in enumerate(outs, 1):
        start = pl.multiple_of(lax.rem(place_ref[0] + step, QUARTERS) * width, width)
        copies.append(
            pltpu.make_async_copy(
                weights_ref.at[:, pl.ds(start, width)], out, sems.at[step - 1]
            )
        )
    run_copies(copies)


def cut(place, weights, width):
    piece = pltpu.VMEM((weights.shape[0], width), weights.dtype)
    return pl.pallas_call(
        cut_kernel,
        out_shape=[piece] * (QUARTERS - 1),
        in_specs=[SMEM, HBM],
        out_specs=[VMEM] * (QUARTERS - 1),
        scratch_shapes=[pltpu.SemaphoreType.DMA((QUARTERS - 1,))],
    )(place, in_hbm(weights))


def in_hbm(value):
    return pltpu.with_memory_space_constraint(value, pltpu.HBM)


def load_kernel(*refs):
    count, sems = len(refs) // 2, refs[-1]
    run_copies(
        [
            copy
            for place in range(count)
            for copy in halves(refs[place], refs[count + place], sems.at[place])
        ]
    )


def loaded(*values):
    return pl.pallas_call(
        load_kernel,
        out_shape=[pltpu.VMEM(v.shape, v.dtype) for v in values],
        in_specs=[HBM] * len(values),
        out_specs=[VMEM] * len(values),
        scratch_shapes=[pltpu.SemaphoreType.DMA((len(values), PARTS))],
        compiler_params=pltpu.CompilerParams(vmem_limit_bytes=2 * 2**20),
    )(*[in_hbm(v) for v in values])


def spread(squares):
    high = squares.astype(BF16)
    low = (squares - high.astype(F32)).astype(BF16)
    row = lax.broadcasted_iota(jnp.int32, (TAIL, squares.shape[1]), 0)
    high, low = high.astype(F32), low.astype(F32)
    return jnp.where(row == 0, high, jnp.where(row == 1, low, 0.0)).astype(BF16)


def hsum_kernel(own_ref, a_ref, b_ref, c_ref, residual_ref, gain_ref, hsum_ref, blocks_ref):
    hsum = (
        residual_ref[...].astype(F32)
        + own_ref[...]
        + a_ref[...].astype(F32)
        + b_ref[...].astype(F32)
        + c_ref[...].astype(F32)
    )
    hsum_ref[...] = hsum
    scaled = (hsum * gain_ref[...].astype(F32)).astype(BF16)
    tail = spread(jnp.sum(hsum * hsum, axis=0, keepdims=True))
    for p in range(PLANE):
        blocks_ref[p, :PAIR, :] = scaled
        blocks_ref[p, PAIR:, :] = tail


def expand_kernel(a_step, b_step, c_step, d_step, *refs):
    weights, blocks_ref, outs = refs[:4], refs[4], refs[5 : 5 + QUARTERS]
    features, sums, buffer, sems = refs[5 + QUARTERS :]
    copies = [
        halves(ref, buffer.at[place], sems.at[place]) for place, ref in enumerate(weights)
    ]
    for group in copies:
        for copy in group:
            copy.start()
    steps = [ref[0] for ref in (a_step, b_step, c_step, d_step)]
    units = weights[0].shape[0] // 2
    squares = jnp.zeros((TAIL, HALF), F32)
    for p in range(PLANE):
        features[p * PAIR : (p + 1) * PAIR, :] = blocks_ref[p, :PAIR, :]
        squares = squares + blocks_ref[p, PAIR:, :].astype(F32)
    tail = spread(squares[0:1] + squares[1:2])
    rows = 2 * units // PARTS
    for place, group in enumerate(copies):
        for part, copy in enumerate(group):
            copy.wait()
            start = place * 2 * units + part * rows
            sums[start : start + rows, :] = jnp.dot(
                buffer[place, part * rows : (part + 1) * rows, :],
                features[...],
                preferred_element_type=F32,
            )
    for part in range(QUARTERS):
        start = (part // 2 * 4 + part % 2) * units
        gates, ups = slice(start, start + units), slice(start + 2 * units, start + 3 * units)
        for step in range(QUARTERS):

            @pl.when(steps[part] == step)
            def _(gates=gates, ups=ups, step=step):
                outs[step][:units, :] = sums[gates, :].astype(BF16)
                outs[step][units : 2 * units, :] = sums[ups, :].astype(BF16)
                outs[step][2 * units :, :] = tail


def hidden_kernel(a_ref, b_ref, c_ref, d_ref, hidden_ref):
    units = hidden_ref.shape[0]
    total = a_ref[...].astype(F32) + b_ref[...].astype(F32)
    total = total + c_ref[...].astype(F32) + d_ref[...].astype(F32)
    squares = total[2 * units : 2 * units + 1] + total[2 * units + 1 : 2 * units + 2]
    inverse = lax.rsqrt(squares / D + 1e-05)
    gate = total[:units] * inverse
    up = total[units : 2 * units] * inverse
    hidden_ref[...] = (gate / (1.0 + jnp.exp(-gate)) * up).astype(BF16)


def contract_kernel(places_ref, own_ref, other_ref, a_ref, b_ref, c_ref, d_ref, out_ref, hidden):
    for step, ref in enumerate((a_ref, b_ref, c_ref, d_ref)):
        start = pl.multiple_of(places_ref[step] * ref.shape[0], 16)
        hidden[pl.ds(start, ref.shape[0]), :] = ref[...]
    values = hidden[...].astype(F32).T.astype(BF16)
    for p in range(0, PLANE, 2):
        columns = slice(p * PAIR, (p + 2) * PAIR)
        rows = jnp.concatenate([own_ref[:, columns], other_ref[:, columns]], 0)
        part = jnp.dot(values, rows, preferred_element_type=F32).astype(BF16)
        out_ref[p] = part[:, :PAIR]
        out_ref[p + 1] = part[:, PAIR:]


def pair_order(own, other, core):
    return jnp.where(
        core == 0, jnp.concatenate([own, other], 0), jnp.concatenate([other, own], 0)
    )


def per_device(
    query,
    key_cache,
    value_cache,
    key_new,
    value_new,
    lengths,
    residual_in,
    out_weight,
    norm_gain,
    gate_weight,
    up_weight,
    down_weight,
):
    core = lax.axis_index("gx") % CORES
    quarter = lax.axis_index("gy")
    order = jnp.asarray(row_order(), BF16)
    width = out_weight.shape[0] // QUARTERS
    columns = out_weight.shape[1]
    half = PLANE * ROWS_HERE

    out_rows = out_weight.T
    own_out = [lax.dynamic_slice_in_dim(out_rows, quarter * width, width, 1)]
    pieces = cut(quarter.astype(jnp.int32).reshape(1), out_rows, width)
    own_out += [along_gy(piece, step) for step, piece in enumerate(pieces, 1)]
    own_out = jnp.concatenate(own_out, 0)

    gate_other, up_other = to_core(gate_weight.T), to_core(up_weight.T)
    down_other = to_core(down_weight)

    residual = jnp.dot(residual_in.T, order, preferred_element_type=F32).astype(BF16)
    gain = jnp.broadcast_to(norm_gain[:, None], (columns, half))
    mine = lax.dynamic_slice_in_dim(residual, core * half, half, 1)
    theirs = lax.dynamic_slice_in_dim(residual, (1 - core) * half, half, 1)
    received = to_core(jnp.concatenate([theirs, gain], 1))
    residual = pair_order(mine, received[:, :half], core)
    gain = pair_order(gain, received[:, half:], core)

    attended = attend(query, key_cache, value_cache, key_new, value_new, lengths)
    gathered = plane_exchange(jnp.broadcast_to(attended[None], (PLANE,) + attended.shape))
    rows = gathered.reshape(half, width)

    other_out = to_core(own_out)

    def project(weights):
        return lax.dot_general(
            weights, rows, (((1,), (1,)), ((), ())), preferred_element_type=F32
        ).reshape(QUARTERS, columns, half)

    own_part, other_part = project(own_out), project(other_out)
    parts = jnp.where(
        core == 0,
        jnp.concatenate([own_part, other_part], 1),
        jnp.concatenate([other_part, own_part], 1),
    )
    sums = [parts[0]] + [
        along_gy(parts[step].astype(BF16), -step) for step in range(1, QUARTERS)
    ]
    hsum, blocks = kernel_call(
        hsum_kernel,
        [
            jax.ShapeDtypeStruct((PAIR, HALF), F32),
            jax.ShapeDtypeStruct((PLANE, PAIR + TAIL, HALF), BF16),
        ],
        scalars=0,
        inputs=6,
    )(*sums, residual, gain)

    steps = [
        ((((part // 2) ^ core) * 2 + part % 2 - quarter) % QUARTERS).reshape(1)
        for part in range(QUARTERS)
    ]
    blocks = plane_exchange(blocks)
    units = gate_weight.shape[1] // 2
    message = jax.ShapeDtypeStruct((2 * units + TAIL, HALF), BF16)
    sends = kernel_call(
        expand_kernel,
        [message] * QUARTERS,
        scratch=[
            pltpu.VMEM((width, HALF), BF16),
            pltpu.VMEM((8 * units, HALF), F32),
            pltpu.VMEM((4, 2 * units, width), BF16),
            pltpu.SemaphoreType.DMA((4, PARTS)),
        ],
        scalars=QUARTERS,
        streamed=4,
        inputs=1,
        limit=22,
    )(
        *steps,
        in_hbm(gate_weight.T),
        in_hbm(up_weight.T),
        in_hbm(gate_other),
        in_hbm(up_other),
        held(blocks),
    )
    sends = [sends[0]] + [along_gy(sends[step], step) for step in range(1, QUARTERS)]
    (hidden,) = kernel_call(
        hidden_kernel, [jax.ShapeDtypeStruct((units, HALF), BF16)], scalars=0, inputs=4
    )(*sends)
    chunks = [hidden] + [along_gy(hidden, step) for step in range(1, QUARTERS)]
    source = (quarter - jnp.arange(QUARTERS, dtype=jnp.int32)) % QUARTERS
    places = ((source // 2) ^ core) * 2 + source % 2
    (branch,) = kernel_call(
        contract_kernel,
        [jax.ShapeDtypeStruct((PLANE, HALF, PAIR), BF16)],
        scratch=[pltpu.VMEM((4 * units, HALF), BF16)],
        inputs=6,
    )(places, *[held(w) for w in loaded(down_weight, down_other)], *chunks)
    branch = jnp.sum(plane_exchange(branch).astype(F32), axis=0)

    out = (hsum + branch.T).astype(BF16)
    mine = lax.dynamic_slice_in_dim(out, core * columns, columns, 0)
    theirs = to_core(lax.dynamic_slice_in_dim(out, (1 - core) * columns, columns, 0))
    out = jnp.where(
        core == 0,
        jnp.concatenate([mine, theirs], 1),
        jnp.concatenate([theirs, mine], 1),
    )
    out = lax.dot_general(order, out, (((1,), (1,)), ((), ())), preferred_element_type=F32)
    return out.astype(BF16)


def solution(mesh):
    placed = (
        P("gx", "gy"),
        P("gx", "gy", None, None),
        P("gx", "gy", None, None),
        P("gx", "gy"),
        P("gx", "gy"),
        P("gx"),
        P(None, ("gy", "gx")),
        P(None, ("gy", "gx")),
        P(("gy", "gx")),
        P("gy", "gx"),
        P("gy", "gx"),
        P("gx", "gy"),
    )
    return jax.shard_map(
        per_device, mesh=mesh, in_specs=placed, out_specs=P(None, ("gy", "gx")), check_vma=False
    )
```

```python
import jax
import jax.numpy as jnp
import numpy as np
from jax import lax
from jax.experimental import pallas as pl
from jax.experimental.pallas import tpu as pltpu
from jax.sharding import PartitionSpec as P

D = 16384
PLANE = 32
CORES = 2
QUARTERS = 4
ROWS_HERE = 4
HALF = PLANE * ROWS_HERE
PAIR = 128
PARTS = 2
TAIL = 16

F32 = jnp.float32
BF16 = jnp.bfloat16


def row_order():
    row = np.arange(PLANE * CORES * ROWS_HERE)
    device, inner = row // ROWS_HERE, row % ROWS_HERE
    place = (device % CORES) * (PLANE * ROWS_HERE) + (device // CORES) * ROWS_HERE + inner
    table = np.zeros((row.size, row.size), np.float32)
    table[row, place] = 1.0
    return table


def to_core(value):
    return lax.ppermute(value, "gx", [(g, g ^ 1) for g in range(PLANE * CORES)])


def along_gy(value, step):
    return lax.ppermute(value, "gy", [(i, (i + step) % QUARTERS) for i in range(QUARTERS)])


def plane_exchange(blocks):
    groups = [[p * CORES + c for p in range(PLANE)] for c in range(CORES)]
    return lax.all_to_all(blocks, "gx", 0, 0, axis_index_groups=groups, tiled=True)


def attend(query, key_cache, value_cache, key_new, value_new, lengths):
    row_count = query.shape[0]
    kv_heads = key_cache.shape[1]
    context = key_cache.shape[2]
    head_size = key_cache.shape[3]
    group_size = query.shape[1] // (kv_heads * head_size)
    query_rows = query.reshape(row_count, kv_heads, group_size, head_size)
    incoming_keys = key_new.reshape(row_count, kv_heads, head_size)
    fresh_values = value_new.astype(F32).reshape(row_count, kv_heads, head_size)
    logit_scale = head_size ** (-0.5)
    cache_scores = (
        jnp.einsum("bkgd,bktd->bkgt", query_rows, key_cache, preferred_element_type=F32)
        * logit_scale
    )
    incoming_scores = (
        jnp.einsum("qaxh,qah->qax", query_rows, incoming_keys, preferred_element_type=F32)
        * logit_scale
    )
    valid = lax.broadcasted_iota(jnp.int32, (row_count, context), 1) < lengths[:, None]
    cache_scores = jnp.where(valid[:, None, None, :], cache_scores, -1e30)
    peak = jnp.maximum(jnp.max(cache_scores, axis=3), incoming_scores)
    cache_weights = jnp.exp(cache_scores - peak[..., None])
    new_weight = jnp.exp(incoming_scores - peak)
    denominator = jnp.sum(cache_weights, axis=3) + new_weight
    cache_low = cache_weights.astype(BF16)
    new_low = new_weight.astype(BF16).astype(F32)
    weighted_value_sum = jnp.einsum(
        "bkgt,bktd->bkgd", cache_low, value_cache, preferred_element_type=F32
    )
    weighted_value_sum = weighted_value_sum + new_low[..., None] * fresh_values[:, :, None, :]
    attended = (weighted_value_sum / denominator[..., None]).astype(BF16)
    return attended.reshape(row_count, kv_heads * group_size * head_size)


VMEM = pl.BlockSpec(memory_space=pltpu.VMEM)
SMEM = pl.BlockSpec(memory_space=pltpu.SMEM)
HBM = pl.BlockSpec(memory_space=pltpu.HBM)


def kernel_call(body, outs, scratch=(), scalars=1, streamed=0, inputs=0, limit=8):
    return pl.pallas_call(
        body,
        out_shape=outs,
        in_specs=[SMEM] * scalars + [HBM] * streamed + [VMEM] * inputs,
        out_specs=[VMEM] * len(outs),
        scratch_shapes=list(scratch),
        compiler_params=pltpu.CompilerParams(vmem_limit_bytes=limit * 2**20),
    )


def held(value):
    return pltpu.with_memory_space_constraint(value, pltpu.VMEM)


def halves(source, target, sems):
    rows = source.shape[0] // PARTS
    return [
        pltpu.make_async_copy(
            source.at[pl.ds(part * rows, rows)], target.at[pl.ds(part * rows, rows)], sems.at[part]
        )
        for part in range(PARTS)
    ]


def run_copies(copies):
    for copy in copies:
        copy.start()
    for copy in copies:
        copy.wait()


def cut_kernel(place_ref, weights_ref, *refs):
    outs, sems = refs[:-1], refs[-1]
    width = outs[0].shape[1]
    copies = []
    for step, out in enumerate(outs, 1):
        start = pl.multiple_of(lax.rem(place_ref[0] + step, QUARTERS) * width, width)
        copies.append(
            pltpu.make_async_copy(
                weights_ref.at[:, pl.ds(start, width)], out, sems.at[step - 1]
            )
        )
    run_copies(copies)


def cut(place, weights, width):
    piece = pltpu.VMEM((weights.shape[0], width), weights.dtype)
    return pl.pallas_call(
        cut_kernel,
        out_shape=[piece] * (QUARTERS - 1),
        in_specs=[SMEM, HBM],
        out_specs=[VMEM] * (QUARTERS - 1),
        scratch_shapes=[pltpu.SemaphoreType.DMA((QUARTERS - 1,))],
    )(place, in_hbm(weights))


def repeat_kernel(value_ref, out_ref):
    for p in range(PLANE):
        out_ref[p] = value_ref[...]


def in_hbm(value):
    return pltpu.with_memory_space_constraint(value, pltpu.HBM)


def load_kernel(*refs):
    count, sems = len(refs) // 2, refs[-1]
    run_copies(
        [
            copy
            for place in range(count)
            for copy in halves(refs[place], refs[count + place], sems.at[place])
        ]
    )


def loaded(*values):
    return pl.pallas_call(
        load_kernel,
        out_shape=[pltpu.VMEM(v.shape, v.dtype) for v in values],
        in_specs=[HBM] * len(values),
        out_specs=[VMEM] * len(values),
        scratch_shapes=[pltpu.SemaphoreType.DMA((len(values), PARTS))],
        compiler_params=pltpu.CompilerParams(vmem_limit_bytes=2 * 2**20),
    )(*[in_hbm(v) for v in values])


def spread(squares):
    high = squares.astype(BF16)
    low = (squares - high.astype(F32)).astype(BF16)
    row = lax.broadcasted_iota(jnp.int32, (TAIL, squares.shape[1]), 0)
    high, low = high.astype(F32), low.astype(F32)
    return jnp.where(row == 0, high, jnp.where(row == 1, low, 0.0)).astype(BF16)


def hsum_kernel(own_ref, a_ref, b_ref, c_ref, residual_ref, gain_ref, hsum_ref, blocks_ref):
    hsum = (
        residual_ref[...].astype(F32)
        + own_ref[...]
        + a_ref[...].astype(F32)
        + b_ref[...].astype(F32)
        + c_ref[...].astype(F32)
    )
    hsum_ref[...] = hsum
    scaled = (hsum * gain_ref[...].astype(F32)).astype(BF16)
    tail = spread(jnp.sum(hsum * hsum, axis=0, keepdims=True))
    for p in range(PLANE):
        blocks_ref[p, :PAIR, :] = scaled
        blocks_ref[p, PAIR:, :] = tail


def expand_kernel(a_step, b_step, c_step, d_step, *refs):
    weights, blocks_ref, outs = refs[:4], refs[4], refs[5 : 5 + QUARTERS]
    features, sums, buffer, sems = refs[5 + QUARTERS :]
    copies = [
        halves(ref, buffer.at[place], sems.at[place]) for place, ref in enumerate(weights)
    ]
    for group in copies:
        for copy in group:
            copy.start()
    steps = [ref[0] for ref in (a_step, b_step, c_step, d_step)]
    units = weights[0].shape[0] // 2
    squares = jnp.zeros((TAIL, HALF), F32)
    for p in range(PLANE):
        features[p * PAIR : (p + 1) * PAIR, :] = blocks_ref[p, :PAIR, :]
        squares = squares + blocks_ref[p, PAIR:, :].astype(F32)
    tail = spread(squares[0:1] + squares[1:2])
    rows = 2 * units // PARTS
    for place, group in enumerate(copies):
        for part, copy in enumerate(group):
            copy.wait()
            start = place * 2 * units + part * rows
            sums[start : start + rows, :] = jnp.dot(
                buffer[place, part * rows : (part + 1) * rows, :],
                features[...],
                preferred_element_type=F32,
            )
    for part in range(QUARTERS):
        start = (part // 2 * 4 + part % 2) * units
        gates, ups = slice(start, start + units), slice(start + 2 * units, start + 3 * units)
        for step in range(QUARTERS):

            @pl.when(steps[part] == step)
            def _(gates=gates, ups=ups, step=step):
                outs[step][:units, :] = sums[gates, :].astype(BF16)
                outs[step][units : 2 * units, :] = sums[ups, :].astype(BF16)
                outs[step][2 * units :, :] = tail


def hidden_kernel(a_ref, b_ref, c_ref, d_ref, hidden_ref):
    units = hidden_ref.shape[0]
    total = a_ref[...].astype(F32) + b_ref[...].astype(F32)
    total = total + c_ref[...].astype(F32) + d_ref[...].astype(F32)
    squares = total[2 * units : 2 * units + 1] + total[2 * units + 1 : 2 * units + 2]
    inverse = lax.rsqrt(squares / D + 1e-05)
    gate = total[:units] * inverse
    up = total[units : 2 * units] * inverse
    hidden_ref[...] = (gate / (1.0 + jnp.exp(-gate)) * up).astype(BF16)


def contract_kernel(places_ref, own_ref, other_ref, a_ref, b_ref, c_ref, d_ref, out_ref, hidden):
    for step, ref in enumerate((a_ref, b_ref, c_ref, d_ref)):
        start = pl.multiple_of(places_ref[step] * ref.shape[0], 16)
        hidden[pl.ds(start, ref.shape[0]), :] = ref[...]
    units = own_ref.shape[0]
    values = [
        hidden[side * units : (side + 1) * units, :].astype(F32).T.astype(BF16)
        for side in range(CORES)
    ]
    for p in range(0, PLANE, 2):
        columns = slice(p * PAIR, (p + 2) * PAIR)
        part = sum(
            jnp.dot(value, ref[:, columns], preferred_element_type=F32)
            for value, ref in zip(values, (own_ref, other_ref))
        ).astype(BF16)
        out_ref[p] = part[:, :PAIR]
        out_ref[p + 1] = part[:, PAIR:]


def pair_order(own, other, core):
    return jnp.where(
        core == 0, jnp.concatenate([own, other], 0), jnp.concatenate([other, own], 0)
    )


def per_device(
    query,
    key_cache,
    value_cache,
    key_new,
    value_new,
    lengths,
    residual_in,
    out_weight,
    norm_gain,
    gate_weight,
    up_weight,
    down_weight,
):
    core = lax.axis_index("gx") % CORES
    quarter = lax.axis_index("gy")
    order = jnp.asarray(row_order(), BF16)
    width = out_weight.shape[0] // QUARTERS
    columns = out_weight.shape[1]
    half = PLANE * ROWS_HERE

    out_rows = out_weight.T
    own_out = [lax.dynamic_slice_in_dim(out_rows, quarter * width, width, 1)]
    pieces = cut(quarter.astype(jnp.int32).reshape(1), out_rows, width)
    own_out += [along_gy(piece, step) for step, piece in enumerate(pieces, 1)]
    own_out = jnp.concatenate(own_out, 0)

    gate_other, up_other = to_core(gate_weight.T), to_core(up_weight.T)
    down_other = to_core(down_weight)

    residual = jnp.dot(residual_in.T, order, preferred_element_type=F32).astype(BF16)
    gain = jnp.broadcast_to(norm_gain[:, None], (columns, half))
    mine = lax.dynamic_slice_in_dim(residual, core * half, half, 1)
    theirs = lax.dynamic_slice_in_dim(residual, (1 - core) * half, half, 1)
    received = to_core(jnp.concatenate([theirs, gain], 1))
    residual = pair_order(mine, received[:, :half], core)
    gain = pair_order(gain, received[:, half:], core)

    attended = attend(query, key_cache, value_cache, key_new, value_new, lengths)
    (attended,) = kernel_call(
        repeat_kernel, [pltpu.VMEM((PLANE,) + attended.shape, BF16)], scalars=0, inputs=1
    )(attended)
    gathered = plane_exchange(attended)
    rows = gathered.reshape(half, width)

    other_out = to_core(own_out)

    def project(weights):
        return lax.dot_general(
            weights, rows, (((1,), (1,)), ((), ())), preferred_element_type=F32
        ).reshape(QUARTERS, columns, half)

    own_part, other_part = project(own_out), project(other_out)
    parts = jnp.where(
        core == 0,
        jnp.concatenate([own_part, other_part], 1),
        jnp.concatenate([other_part, own_part], 1),
    )
    sums = [parts[0]] + [
        along_gy(parts[step].astype(BF16), -step) for step in range(1, QUARTERS)
    ]
    hsum, blocks = kernel_call(
        hsum_kernel,
        [
            jax.ShapeDtypeStruct((PAIR, HALF), F32),
            pltpu.VMEM((PLANE, PAIR + TAIL, HALF), BF16),
        ],
        scalars=0,
        inputs=6,
    )(*sums, residual, gain)

    steps = [
        ((((part // 2) ^ core) * 2 + part % 2 - quarter) % QUARTERS).reshape(1)
        for part in range(QUARTERS)
    ]
    blocks = plane_exchange(blocks)
    units = gate_weight.shape[1] // 2
    message = jax.ShapeDtypeStruct((2 * units + TAIL, HALF), BF16)
    sends = kernel_call(
        expand_kernel,
        [message] * QUARTERS,
        scratch=[
            pltpu.VMEM((width, HALF), BF16),
            pltpu.VMEM((8 * units, HALF), F32),
            pltpu.VMEM((4, 2 * units, width), BF16),
            pltpu.SemaphoreType.DMA((4, PARTS)),
        ],
        scalars=QUARTERS,
        streamed=4,
        inputs=1,
        limit=22,
    )(
        *steps,
        in_hbm(gate_weight.T),
        in_hbm(up_weight.T),
        in_hbm(gate_other),
        in_hbm(up_other),
        held(blocks),
    )
    sends = [sends[0]] + [along_gy(sends[step], step) for step in range(1, QUARTERS)]
    (hidden,) = kernel_call(
        hidden_kernel, [jax.ShapeDtypeStruct((units, HALF), BF16)], scalars=0, inputs=4
    )(*sends)
    chunks = [hidden] + [along_gy(hidden, step) for step in range(1, QUARTERS)]
    source = (quarter - jnp.arange(QUARTERS, dtype=jnp.int32)) % QUARTERS
    places = ((source // 2) ^ core) * 2 + source % 2
    (branch,) = kernel_call(
        contract_kernel,
        [pltpu.VMEM((PLANE, HALF, PAIR), BF16)],
        scratch=[pltpu.VMEM((4 * units, HALF), BF16)],
        inputs=6,
    )(places, *[held(w) for w in loaded(down_weight, down_other)], *chunks)
    branch = jnp.sum(plane_exchange(branch).astype(F32), axis=0)

    out = (hsum + branch.T).astype(BF16)
    mine = lax.dynamic_slice_in_dim(out, core * columns, columns, 0)
    theirs = to_core(lax.dynamic_slice_in_dim(out, (1 - core) * columns, columns, 0))
    out = jnp.where(
        core == 0,
        jnp.concatenate([mine, theirs], 1),
        jnp.concatenate([theirs, mine], 1),
    )
    out = lax.dot_general(order, out, (((1,), (1,)), ((), ())), preferred_element_type=F32)
    return out.astype(BF16)


def solution(mesh):
    placed = (
        P("gx", "gy"),
        P("gx", "gy", None, None),
        P("gx", "gy", None, None),
        P("gx", "gy"),
        P("gx", "gy"),
        P("gx"),
        P(None, ("gy", "gx")),
        P(None, ("gy", "gx")),
        P(("gy", "gx")),
        P("gy", "gx"),
        P("gy", "gx"),
        P("gx", "gy"),
    )
    return jax.shard_map(
        per_device, mesh=mesh, in_specs=placed, out_specs=P(None, ("gy", "gx")), check_vma=False
    )
```
